32 devices in a mesh: coord: 8 (over z, x), dp: 4 (over y, core).
Axes of the slice: x: 2, y: 2, z: 4, core: 2. Of those that a mesh axis runs over, the one named last changes fastest.
Arguments:
- h_train: bfloat16 [2, 512, 256, 128], P(None, 'dp'), may hold values from -6 to 6
- gout_train: bfloat16 [2, 512, 256, 5120], P(None, 'dp', None, 'coord'), may hold values from -96 to 96
- h_val: bfloat16 [2, 64, 256, 128], P(None, 'dp'), may hold values from -6 to 6
- gout_val: bfloat16 [2, 64, 256, 5120], P(None, 'dp', None, 'coord'), may hold values from -96 to 96
- proj: bfloat16 [2, 5120, 128, 128], P(None, 'coord'), may hold values from -0.0390625 to 0.0390625
- bins: int32 [2, 5120], P(None, 'coord'), may hold values from 0 to 63
- tasks: int32 [64, 1], replicated, may hold values from 0 to 2
Outputs:
- cosines: float32 [512, 64], P('dp')
- scores: float32 [512, 3], P('dp')
The draws below stay inside these ranges and needn't reach their ends.
Inputs may be any that keep to these rules, and one draw needn't show every extreme that they name: `tasks`: every one of the 3 benchmarks has at least one validation example.
All inputs are finite; a program needn't handle non-finite values.
Results may differ from the reference program's by a relative error of at most 0.0003.
Values sent between devices are 32-bit elements; how exact they have to be, the bound alone decides.
A program may use at most 384 MiB of HBM per device.

```python
import math
import jax
import jax.numpy as jnp
from jax import lax

DOUT = 5120
R = 128
KPROJ = 8192
BW = 128
LAYERS = 2
TOK = 256
NTASK = 3
NBIN = 64
TRAIN = 512
VAL = 64


def common_tokens(key, salt, width):
    return jax.random.normal(jax.random.fold_in(key, salt), (LAYERS, 1, TOK, width), jnp.float32)


def mixture(common, own, weight):
    return jnp.clip(weight * common + math.sqrt(1.0 - weight * weight) * own, -6.0, 6.0)


def draw_h_train(key, part):
    common = common_tokens(key, 501, R)
    key = jax.random.fold_in(key, 1)
    own = jax.random.normal(key, (LAYERS, TRAIN, TOK, R), jnp.float32)
    return mixture(common, own, 0.75).astype(jnp.bfloat16)


def draw_h_val(key, part):
    common = common_tokens(key, 501, R)
    key = jax.random.fold_in(key, 2)
    own = jax.random.normal(key, (LAYERS, VAL, TOK, R), jnp.float32)
    return mixture(common, own, 0.75).astype(jnp.bfloat16)


def draw_gout_train(key, part):
    common = common_tokens(key, 502, DOUT)
    key = jax.random.fold_in(key, 3)
    own = jax.random.normal(jax.random.fold_in(key, 7), (LAYERS, TRAIN, TOK, DOUT), jnp.float32)
    spread = jnp.exp(jax.random.uniform(jax.random.fold_in(key, 8), (LAYERS, TRAIN, 1, 1), jnp.float32, 0.0, math.log(10.0)))
    return (mixture(common, own, 0.75) * spread).astype(jnp.bfloat16)


def draw_gout_val(key, part):
    common = common_tokens(key, 502, DOUT)
    key = jax.random.fold_in(key, 4)
    own = jax.random.normal(jax.random.fold_in(key, 7), (LAYERS, VAL, TOK, DOUT), jnp.float32)
    spread = jnp.exp(jax.random.uniform(jax.random.fold_in(key, 8), (LAYERS, VAL, 1, 1), jnp.float32, 0.0, math.log(10.0)))
    return (mixture(common, own, 0.75) * spread).astype(jnp.bfloat16)


def with_ends(array, key, least, largest):
    index_at = [jax.random.randint(jax.random.fold_in(key, axis), (), 0, length) for axis, length in enumerate(array.shape)]
    main_axis = array.shape.index(max(array.shape))
    next_to = index_at[:main_axis] + [(index_at[main_axis] + 1) % array.shape[main_axis]] + index_at[main_axis + 1:]
    return array.at[tuple(index_at)].set(least).at[tuple(next_to)].set(largest)


def levels(rng, dims, pieces, low, high):
    level = 1.0
    for dim, shards_of in pieces:
        draws = jax.random.uniform(jax.random.fold_in(jax.random.fold_in(rng, 6), dim), (shards_of,), jnp.float32, low / len(pieces), high / len(pieces))
        level = level * jnp.repeat(jnp.exp(draws), dims[dim] // shards_of).reshape((-1,) + (1,) * (len(dims) - 1 - dim))
    return level


def distinct(stream_key, rows, amount, top, lift):
    sequence = jax.random.permutation(jax.random.fold_in(stream_key, 1), amount)
    favour = sequence
    for power in range(3):
        favour = favour * favour // amount
    favour = favour * lift // amount
    lots = jax.random.randint(jax.random.fold_in(stream_key, 2), (rows, amount), 0, 4096) + favour
    holders = jax.random.permutation(jax.random.fold_in(stream_key, 3), rows)[jnp.arange(amount) % rows]
    lots = jnp.where(jnp.arange(rows)[:, None] == holders[None, :], 1 << 14, lots)
    merit = lots * amount + jnp.arange(amount)
    return lax.top_k(merit.astype(jnp.int32), top)[1].astype(jnp.int32)


def noise(own_key, extent, scale, most, cuts=(), dtype=jnp.bfloat16):
    level = levels(own_key, extent, cuts, -0.22, 0.18) if cuts else 1.0
    array = jax.random.normal(own_key, extent, jnp.float32) * scale * level
    return jnp.minimum(jnp.maximum(array, -most), most).astype(dtype)


def setup_inputs(seed: int = 0) -> dict:
    arg_keys = jax.random.split(jax.random.key(seed), 8)
    return {
        "h_train": draw_h_train(jax.random.fold_in(arg_keys[7], 71), 0),
        "gout_train": draw_gout_train(jax.random.fold_in(arg_keys[7], 71), 0),
        "h_val": draw_h_val(jax.random.fold_in(arg_keys[7], 71), 0),
        "gout_val": draw_gout_val(jax.random.fold_in(arg_keys[7], 71), 0),
        "proj": noise(arg_keys[4], (LAYERS, DOUT, R, BW), (R * DOUT * LAYERS // NBIN) ** -0.5, 0.0390625, ((1, 8),)),
        "bins": with_ends(jax.random.randint(arg_keys[5], (LAYERS, DOUT), 0, NBIN), jax.random.fold_in(arg_keys[5], 1), 0, NBIN - 1).astype(jnp.int32),
        "tasks": distinct(arg_keys[6], VAL, NTASK, 1, 0),
    }


def features_of(h_all, g_all, proj, bins):
    total = jnp.zeros((h_all.shape[1], NBIN, BW), jnp.float32)
    for layer in range(LAYERS):
        weights = proj[layer].astype(jnp.float32)
        onehot = (bins[layer][:, None] == jnp.arange(NBIN)[None, :]).astype(jnp.float32)

        def one_example(pair):
            hx, gx = pair
            grads = jnp.dot(gx.T, hx, preferred_element_type=jnp.float32).astype(jnp.bfloat16)
            placed = jnp.einsum('jr,jrk->jk', grads.astype(jnp.float32), weights, precision=lax.Precision.HIGHEST)
            return jnp.dot(onehot.T, placed, precision=lax.Precision.HIGHEST)
        total = total + lax.map(one_example, (h_all[layer], g_all[layer]))
    return total.reshape(h_all.shape[1], KPROJ)

def reference(h_train, gout_train, h_val, gout_val, proj, bins, tasks):
    train_feats = features_of(h_train, gout_train, proj, bins)
    val_feats = features_of(h_val, gout_val, proj, bins)
    train_norm = jnp.sqrt(lax.optimization_barrier(jnp.sum(train_feats * train_feats, axis=1)) + 1e-06)
    val_norm = jnp.sqrt(lax.optimization_barrier(jnp.sum(val_feats * val_feats, axis=1)) + 1e-06)
    dots = jnp.dot(train_feats, val_feats.T, precision=lax.Precision.HIGHEST)
    cosines = dots / (train_norm[:, None] * val_norm[None, :])
    members = (tasks[:, 0][:, None] == jnp.arange(NTASK)[None, :]).astype(jnp.float32)
    scores = jnp.dot(cosines, members, precision=lax.Precision.HIGHEST) / lax.optimization_barrier(jnp.sum(members, axis=0))[None, :]
    return (cosines, scores)
```

```python
import functools

import jax
import jax.numpy as jnp
from jax import lax
from jax.experimental import pallas as pl
from jax.experimental.pallas import tpu as pltpu
from jax.sharding import PartitionSpec as P

KPROJ = 8192
BW = 128
NTASK = 3
NBIN = KPROJ // BW
SUB = 8
STRIDE = SUB + 1


def features_kernel(width, n_sets, bins_ref, *refs):
    pairs = [(refs[2 * s], refs[2 * s + 1]) for s in range(n_sets)]
    proj_ref, out_ref, grads_ref = refs[2 * n_sets :]
    layer, block = pl.program_id(0), pl.program_id(1)
    n_blocks = pl.num_programs(1)
    groups = grads_ref.shape[0]

    @pl.when((layer == 0) & (block == 0))
    def _():
        out_ref[...] = jnp.zeros_like(out_ref)

    first = 0
    for g_ref, h_ref in pairs:
        n_groups = g_ref.shape[1] // SUB

        def one_group(group, carry, g_ref=g_ref, h_ref=h_ref, first=first):
            for i in range(SUB):
                e = group * SUB + i
                grads = lax.dot_general(
                    g_ref[0, e],
                    h_ref[0, e],
                    (((0,), (0,)), ((), ())),
                    preferred_element_type=jnp.float32,
                )
                for jj in range(width // SUB):
                    grads_ref[first + group, jj, pl.ds(i * STRIDE, SUB), :] = grads[
                        jj * SUB : (jj + 1) * SUB
                    ]
            return carry

        lax.fori_loop(0, n_groups, one_group, 0)
        first += n_groups

    base = (layer * n_blocks + block) * width

    def columns(jj, carry):
        placed = []
        for i in range(SUB):
            rows = jnp.concatenate(
                [grads_ref[group, jj, pl.ds(i, SUB, stride=STRIDE), :] for group in range(groups)],
                axis=0,
            ).astype(jnp.bfloat16)
            placed.append(
                jnp.dot(rows, proj_ref[0, jj * SUB + i], preferred_element_type=jnp.float32)
            )
            if len(placed) == 4:
                for k in range(4):
                    b = bins_ref[base + jj * SUB + i - 3 + k]
                    out_ref[b] += placed[k]
                placed = []
        return carry

    lax.fori_loop(0, width // SUB, columns, 0)


def features(bins, proj, sets):
    layers, columns = proj.shape[0], proj.shape[1]
    width = 128 if columns % 128 == 0 else columns
    examples = sum(size for _, _, size, _ in sets)
    in_specs, operands = [], []
    for g, h, size, at in sets:
        in_specs.append(
            pl.BlockSpec((1, size, g.shape[2], width), lambda l, j, b, at=at: (l, at, 0, j))
        )
        in_specs.append(
            pl.BlockSpec((1, size, h.shape[2], h.shape[3]), lambda l, j, b, at=at: (l, at, 0, 0))
        )
        operands += [g, h]
    in_specs.append(
        pl.BlockSpec((1, width, proj.shape[2], BW), lambda l, j, b: (l, j, 0, 0))
    )
    tok, rank = sets[0][1].shape[2:]
    flops = 2 * layers * examples * columns * rank * (tok + BW)
    moved = 2 * layers * (examples * tok * (columns + rank) + columns * rank * BW)
    return pl.pallas_call(
        functools.partial(features_kernel, width, len(sets)),
        grid_spec=pltpu.PrefetchScalarGridSpec(
            num_scalar_prefetch=1,
            grid=(layers, columns // width),
            in_specs=in_specs,
            out_specs=pl.BlockSpec((NBIN, examples, BW), lambda l, j, b: (0, 0, 0)),
            scratch_shapes=[
                pltpu.VMEM((examples // SUB, width // SUB, SUB * STRIDE, rank), jnp.float32)
            ],
        ),
        out_shape=jax.ShapeDtypeStruct((NBIN, examples, BW), jnp.float32),
        compiler_params=pltpu.CompilerParams(
            dimension_semantics=("arbitrary", "arbitrary"), vmem_limit_bytes=60 * 1024 * 1024
        ),
        cost_estimate=pl.CostEstimate(flops=flops, bytes_accessed=moved, transcendentals=0),
    )(bins.reshape(-1), *operands, proj)


def per_device(h_train, gout_train, h_val, gout_val, proj, bins, tasks):
    n_train, n_val = h_train.shape[1], h_val.shape[1]
    half = n_train // 2
    first = features(
        bins, proj, [(gout_train, h_train, half, 0), (gout_val, h_val, n_val, 0)]
    )
    second = features(bins, proj, [(gout_train, h_train, half, 1)])
    first = lax.psum_scatter(first, "coord", scatter_dimension=0, tiled=True)
    second = lax.psum_scatter(second, "coord", scatter_dimension=0, tiled=True)
    val = lax.all_gather(first[:, half:], "dp", axis=1, tiled=True)

    def against(rows):
        dots = jnp.einsum("bek,bvk->ev", rows, val, precision=lax.Precision.HIGHEST)
        return dots, jnp.sum(rows * rows, axis=(0, 2))

    parts = [against(first[:, :half]), against(second)]
    val_sq = jnp.sum(val * val, axis=(0, 2))
    dots = jnp.concatenate([p[0] for p in parts], axis=0)
    train_sq = jnp.concatenate([p[1] for p in parts], axis=0)
    dots, train_sq, val_sq = lax.psum((dots, train_sq, val_sq), "coord")
    train_norm = jnp.sqrt(train_sq + 1e-06)
    val_norm = jnp.sqrt(val_sq + 1e-06)
    cosines = dots / (train_norm[:, None] * val_norm[None, :])
    members = (tasks[:, 0][:, None] == jnp.arange(NTASK)[None, :]).astype(jnp.float32)
    scores = (
        jnp.dot(cosines, members, precision=lax.Precision.HIGHEST)
        / jnp.sum(members, axis=0)[None, :]
    )
    return (cosines, scores)


def solution(mesh):
    in_specs = (
        P(None, "dp", None, None),
        P(None, "dp", None, "coord"),
        P(None, "dp", None, None),
        P(None, "dp", None, "coord"),
        P(None, "coord", None, None),
        P(None, "coord"),
        P(),
    )
    out_specs = (P("dp", None), P("dp", None))
    return jax.shard_map(
        per_device, mesh=mesh, in_specs=in_specs, out_specs=out_specs, check_vma=False
    )
```

```python
import functools

import jax
import jax.numpy as jnp
from jax import lax
from jax.experimental import pallas as pl
from jax.experimental.pallas import tpu as pltpu
from jax.sharding import PartitionSpec as P

KPROJ = 8192
BW = 128
NTASK = 3
NBIN = KPROJ // BW
SUB = 8
STRIDE = SUB + 1


def features_kernel(width, n_sets, bins_ref, *refs):
    pairs = [(refs[2 * s], refs[2 * s + 1]) for s in range(n_sets)]
    proj_ref, out_ref, grads_ref = refs[2 * n_sets :]
    layer, block = pl.program_id(0), pl.program_id(1)
    n_blocks = pl.num_programs(1)
    groups = grads_ref.shape[0]

    @pl.when((layer == 0) & (block == 0))
    def _():
        out_ref[...] = jnp.zeros_like(out_ref)

    first = 0
    for g_ref, h_ref in pairs:
        n_groups = g_ref.shape[1] // SUB

        def one_group(group, carry, g_ref=g_ref, h_ref=h_ref, first=first):
            for i in range(SUB):
                e = group * SUB + i
                grads = lax.dot_general(
                    g_ref[0, e],
                    h_ref[0, e],
                    (((0,), (0,)), ((), ())),
                    preferred_element_type=jnp.float32,
                )
                for jj in range(width // SUB):
                    grads_ref[first + group, jj, pl.ds(i * STRIDE, SUB), :] = grads[
                        jj * SUB : (jj + 1) * SUB
                    ]
            return carry

        lax.fori_loop(0, n_groups, one_group, 0)
        first += n_groups

    base = (layer * n_blocks + block) * width

    def columns(jj, carry):
        placed = []
        for i in range(SUB):
            rows = jnp.concatenate(
                [grads_ref[group, jj, pl.ds(i, SUB, stride=STRIDE), :] for group in range(groups)],
                axis=0,
            ).astype(jnp.bfloat16)
            placed.append(
                jnp.dot(rows, proj_ref[0, jj * SUB + i], preferred_element_type=jnp.float32)
            )
            if len(placed) == 4:
                for k in range(4):
                    b = bins_ref[base + jj * SUB + i - 3 + k]
                    out_ref[b] += placed[k]
                placed = []
        return carry

    lax.fori_loop(0, width // SUB, columns, 0)


def features(bins, proj, sets):
    layers, columns = proj.shape[0], proj.shape[1]
    width = 128 if columns % 128 == 0 else columns
    examples = sum(size for _, _, size, _ in sets)
    in_specs, operands = [], []
    for g, h, size, at in sets:
        in_specs.append(
            pl.BlockSpec((1, size, g.shape[2], width), lambda l, j, b, at=at: (l, at, 0, j))
        )
        in_specs.append(
            pl.BlockSpec((1, size, h.shape[2], h.shape[3]), lambda l, j, b, at=at: (l, at, 0, 0))
        )
        operands += [g, h]
    in_specs.append(
        pl.BlockSpec((1, width, proj.shape[2], BW), lambda l, j, b: (l, j, 0, 0))
    )
    tok, rank = sets[0][1].shape[2:]
    flops = 2 * layers * examples * columns * rank * (tok + BW)
    moved = 2 * layers * (examples * tok * (columns + rank) + columns * rank * BW)
    return pl.pallas_call(
        functools.partial(features_kernel, width, len(sets)),
        grid_spec=pltpu.PrefetchScalarGridSpec(
            num_scalar_prefetch=1,
            grid=(layers, columns // width),
            in_specs=in_specs,
            out_specs=pl.BlockSpec((NBIN, examples, BW), lambda l, j, b: (0, 0, 0)),
            scratch_shapes=[
                pltpu.VMEM((examples // SUB, width // SUB, SUB * STRIDE, rank), jnp.float32)
            ],
        ),
        out_shape=jax.ShapeDtypeStruct((NBIN, examples, BW), jnp.float32),
        compiler_params=pltpu.CompilerParams(
            dimension_semantics=("arbitrary", "arbitrary"), vmem_limit_bytes=60 * 1024 * 1024
        ),
        cost_estimate=pl.CostEstimate(flops=flops, bytes_accessed=moved, transcendentals=0),
    )(bins.reshape(-1), *operands, proj)


def per_device(h_train, gout_train, h_val, gout_val, proj, bins, tasks):
    n_train, n_val = h_train.shape[1], h_val.shape[1]
    half, quarter = n_train // 2, n_train // 4
    sets = [
        [(gout_train, h_train, half, 0)],
        [(gout_train, h_train, quarter, 2), (gout_val, h_val, n_val, 0)],
        [(gout_train, h_train, quarter, 3)],
    ]
    sums = []
    for group in sets:
        if sums:
            bins, _ = lax.optimization_barrier((bins, local))
        local = features(bins, proj, group)
        sums.append(local)
    for i in range(len(sums)):
        if i:
            sums[i], sums[i - 1] = lax.optimization_barrier((sums[i], sums[i - 1]))
        sums[i] = lax.psum_scatter(sums[i], "coord", scatter_dimension=0, tiled=True)
    val = lax.all_gather(sums[1][:, quarter:], "dp", axis=1, tiled=True)

    def against(rows):
        dots = jnp.einsum("bek,bvk->ev", rows, val, precision=lax.Precision.HIGHEST)
        return dots, jnp.sum(rows * rows, axis=(0, 2))

    parts = [against(rows) for rows in (sums[0], sums[1][:, :quarter], sums[2])]
    dots = jnp.concatenate([p[0] for p in parts], axis=0)
    train_sq = jnp.concatenate([p[1] for p in parts], axis=0)
    val_sq = jnp.sum(val * val, axis=(0, 2))
    n_all = dots.shape[1]
    lanes = -(-(n_all + 1) // 128) * 128
    packed = jnp.concatenate([dots, train_sq[:, None]], axis=1)
    packed = jnp.pad(packed, ((0, 8), (0, lanes - n_all - 1)))
    packed = packed + jnp.pad(val_sq[None, :], ((n_train, 7), (0, lanes - n_all)))
    packed = jnp.sum(lax.all_gather(packed, "coord", axis=0), axis=0)
    dots, train_sq, val_sq = (
        packed[:n_train, :n_all],
        packed[:n_train, n_all],
        packed[n_train, :n_all],
    )
    train_norm = jnp.sqrt(train_sq + 1e-06)
    val_norm = jnp.sqrt(val_sq + 1e-06)
    cosines = dots / (train_norm[:, None] * val_norm[None, :])
    members = (tasks[:, 0][:, None] == jnp.arange(NTASK)[None, :]).astype(jnp.float32)
    scores = (
        jnp.dot(cosines, members, precision=lax.Precision.HIGHEST)
        / jnp.sum(members, axis=0)[None, :]
    )
    return (cosines, scores)


def solution(mesh):
    in_specs = (
        P(None, "dp", None, None),
        P(None, "dp", None, "coord"),
        P(None, "dp", None, None),
        P(None, "dp", None, "coord"),
        P(None, "coord", None, None),
        P(None, "coord"),
        P(),
    )
    out_specs = (P("dp", None), P("dp", None))
    return jax.shard_map(
        per_device, mesh=mesh, in_specs=in_specs, out_specs=out_specs, check_vma=False
    )
```
